128 devices in a mesh: tm: 2 (over core), layer: 2 (over x_lo), mode: 32 (over z, y, x_hi).
Axes of the slice: x: 4 (x_hi: 2, x_lo: 2; x = x_hi * 2 + x_lo), y: 4, z: 4, core: 2. Of those that a mesh axis runs over, the one named last changes fastest.
Arguments:
- innovation: bfloat16 [2, 2, 32, 2048, 2048], P(None, 'layer', 'tm', 'mode'), may hold values from -6 to 6
- retention: float32 [2, 2048, 2048], P('layer', 'mode'), may hold values from 0.8 to 0.999
- rytov_filter: float32 [2, 2048, 2048], P('layer', 'mode'), may hold values from 0.1 to 1
- wind_shift: float32 [2, 32, 2], P('layer', 'tm'), may hold values from -3 to 3
- start_state: float32 [2, 2, 2048, 2048], P(None, 'layer', 'mode'), may hold values from -8 to 8
Outputs:
- log_amplitude: float32 [32, 2048, 2048], P(('tm', 'layer'), 'mode')
The draws below stay inside these ranges and needn't reach their ends.
All inputs are finite; a program needn't handle non-finite values.
Results may differ from the reference program's by a relative error of at most 0.014.
Values may be sent and summed in bfloat16 or wider, within the bound.
No kernel may reach another device: no remote copies, remote signals or barrier semaphores. Data moves between devices by JAX's collectives and lax.ppermute only.
A program may use at most 128 MiB of HBM per device.

```python
import math
import jax
import jax.numpy as jnp
from jax import lax

NK = 2048
LAYERS = 2
STEPS = 32


def block_levels(rng, dims, cuts, low, largest):
    factor_of, own = 1.0, jax.random.fold_in(rng, 6)
    for dim, shards_of in cuts:
        heights = jnp.exp(jax.random.uniform(jax.random.fold_in(own, dim), (shards_of,), jnp.float32, low / len(cuts), largest / len(cuts)))
        factor_of = factor_of * jnp.repeat(heights, dims[dim] // shards_of).reshape([-1 if axis == dim else 1 for axis in range(len(dims))])
    return factor_of


def bell_draw(own_key, extent, width, bound, shards=(), kind=jnp.bfloat16):
    array = jax.random.normal(own_key, extent, jnp.float32) * width
    if len(shards) > 0:
        array = block_levels(own_key, extent, shards, -0.22, 0.18) * array
    return jnp.clip(array, min=-bound, max=bound).astype(kind)


def setup_inputs(seed: int = 0) -> dict:
    keys = jax.random.split(jax.random.key(seed), 6)
    innovation = bell_draw(keys[0], (2, LAYERS, STEPS, NK, NK), 1.0, 6.0, ((1, 2), (2, 2), (3, 32)))
    retention = jnp.clip(jnp.exp(math.log(0.999) - 0.22214305 * jax.random.uniform(keys[1], (LAYERS, NK, NK), jnp.float32) ** block_levels(keys[1], (LAYERS, NK, NK), ((0, 2), (1, 32)), -0.2, 0.2)), 0.8, 0.999)
    rytov_filter = jnp.clip(jnp.exp(math.log(1.0) - 2.3025851 * jax.random.uniform(keys[2], (LAYERS, NK, NK), jnp.float32) ** block_levels(keys[2], (LAYERS, NK, NK), ((0, 2), (1, 32)), -0.2, 0.2)), 0.1, 1.0)
    wind_shift = jnp.clip(jax.random.uniform(keys[3], (LAYERS, STEPS, 2), jnp.float32, -3.0, 3.0) * block_levels(keys[3], (LAYERS, STEPS, 2), ((0, 2), (1, 2)), -0.4, 0.0), -3.0, 3.0)
    start_state = bell_draw(keys[4], (2, LAYERS, NK, NK), 2.0, 8.0, ((1, 2), (2, 32)), jnp.float32)
    return {"innovation": innovation, "retention": retention, "rytov_filter": rytov_filter, "wind_shift": wind_shift, "start_state": start_state}


def signed_wave(grid_size):
    indices = jnp.arange(grid_size, dtype=jnp.int32)
    return jnp.where(indices >= grid_size // 2, indices - grid_size, indices).astype(jnp.float32)


def dft_tables(grid_size):
    indices = jnp.arange(grid_size, dtype=jnp.int32)
    product = (indices[:, None] * indices[None, :]) % grid_size
    phase_grid = product.astype(jnp.float32) * (2.0 * math.pi / grid_size)
    return jnp.cos(phase_grid), jnp.sin(phase_grid)


def exact_dot(left_side, right_side):
    return jnp.dot(left_side.astype(jnp.float32), right_side.astype(jnp.float32),
                   precision=lax.Precision.HIGHEST)


def reference(innovation, retention, rytov_filter, wind_shift, start_state):
    grid_size = NK
    wave_x = signed_wave(grid_size)[None, :, None]
    wave_y = signed_wave(grid_size)[None, None, :]
    angle_step = 2.0 * math.pi / grid_size
    cos_table, sin_table = dft_tables(grid_size)
    cos_low = cos_table.astype(jnp.bfloat16)
    sin_low = sin_table.astype(jnp.bfloat16)
    inverse = 1.0 / grid_size

    def advance(running, step_index):
        real_state, imag_state = running
        noise_step = lax.dynamic_index_in_dim(innovation, step_index, 2, False)
        wind_step = lax.dynamic_index_in_dim(wind_shift, step_index, 1, False)
        phase_angle = (wave_x * wind_step[:, 0, None, None] + wave_y * wind_step[:, 1, None, None]) * angle_step
        gain_real = retention * jnp.cos(phase_angle)
        gain_imag = retention * jnp.sin(phase_angle)
        next_real = gain_real * real_state - gain_imag * imag_state + noise_step[0].astype(jnp.float32)
        next_imag = gain_real * imag_state + gain_imag * real_state + noise_step[1].astype(jnp.float32)
        low_real = lax.optimization_barrier((rytov_filter * next_real).astype(jnp.bfloat16))
        low_imag = lax.optimization_barrier((rytov_filter * next_imag).astype(jnp.bfloat16))
        spec_real = jnp.sum(low_real.astype(jnp.float32), axis=0).astype(jnp.bfloat16)
        spec_imag = jnp.sum(low_imag.astype(jnp.float32), axis=0).astype(jnp.bfloat16)
        half_real = exact_dot(spec_real, cos_low) - exact_dot(spec_imag, sin_low)
        half_imag = exact_dot(spec_real, sin_low) + exact_dot(spec_imag, cos_low)
        real_low = lax.optimization_barrier(half_real.astype(jnp.bfloat16))
        imag_low = lax.optimization_barrier(half_imag.astype(jnp.bfloat16))
        frame_out = (exact_dot(real_low.T, cos_low) - exact_dot(imag_low.T, sin_low)) * inverse
        return (next_real, next_imag), frame_out

    step_list = jnp.arange(STEPS, dtype=jnp.int32)
    last_state, frames = lax.scan(advance, (start_state[0], start_state[1]), step_list)
    return frames
```

```python
import math

import jax
import jax.numpy as jnp
import numpy as np
from jax import lax
from jax.experimental import pallas as pl
from jax.experimental.pallas import tpu as pltpu
from jax.sharding import PartitionSpec as P

F32, BF16 = jnp.float32, jnp.bfloat16
ROWS = 16
VMEM = 56 * 1024 * 1024


def trig(n):
    k = np.arange(n, dtype=np.int64)
    prod = (k[:, None] * k[None, :]) % n
    ang = np.arange(n, dtype=np.float64) * (2.0 * math.pi / n)
    return np.cos(ang)[prod], np.sin(ang)[prod]


def tables(n, parts):
    cos, sin = trig(n)
    half, slab = n // 2, n // parts
    rows = np.concatenate([cos[:, :half], -sin[:, :half]], 1)
    first = rows.reshape(half, 2, n).transpose(1, 0, 2)
    second = np.stack(
        [cos.reshape(parts, slab, n), -sin.reshape(parts, slab, n)], 1
    ).reshape(2 * n, n) * (1.0 / n)
    bf = jnp.bfloat16
    return first.astype(bf), second.astype(bf)


def scan_kernel(flag, enter, noise, keep, filt, ea, eb, *rest):
    z, last = rest[-2:]
    steps = noise.shape[1]
    n = noise.shape[3]
    half = n // 2

    @pl.when(flag[0] == 1)
    def _():
        def lanes(j, carry):
            at = [pl.ds(pl.multiple_of(j * 128 + h * half, 128), 128) for h in range(2)]
            re = [enter[0, :, c].astype(F32) for c in at]
            im = [enter[1, :, c].astype(F32) for c in at]
            kp = [keep[:, c] for c in at]
            ft = [filt[:, c] for c in at]
            for t in range(steps):
                ar, ai = ea[0, t], ea[1, t]
                tr, ti = [], []
                for h in range(2):
                    br, bi = eb[0, t : t + 1, at[h]], eb[1, t : t + 1, at[h]]
                    gr = kp[h] * (ar * br - ai * bi)
                    gi = kp[h] * (ar * bi + ai * br)
                    nr = gr * re[h] - gi * im[h] + noise[0, t, :, at[h]].astype(F32)
                    ni = gr * im[h] + gi * re[h] + noise[1, t, :, at[h]].astype(F32)
                    re[h], im[h] = nr, ni
                    tr.append(ft[h] * nr)
                    ti.append(ft[h] * ni)
                for p in range(2):
                    pr = tr[0] + tr[1] if p == 0 else tr[0] - tr[1]
                    pi = ti[0] + ti[1] if p == 0 else ti[0] - ti[1]
                    z[p, t, 0, :, at[0]] = pr.astype(BF16)
                    z[p, t, 0, :, at[1]] = pi.astype(BF16)
                    z[p, t, 1, :, at[0]] = pi.astype(BF16)
                    z[p, t, 1, :, at[1]] = (-pr).astype(BF16)
            for h in range(2):
                last[0, :, at[h]] = re[h].astype(BF16)
                last[1, :, at[h]] = im[h].astype(BF16)
            return carry

        lax.fori_loop(0, half // 128, lanes, 0)


def scan_call(flag, enter, noise, keep, filt, ea, eb, z=None):
    steps, slab, n = noise.shape[1:]
    blocks = slab // ROWS

    def src(i, f):
        return jnp.where(f[0] == 1, i, 0)

    def dst(i, f):
        return jnp.where(f[0] == 1, i, blocks)

    in_specs = [
        pl.BlockSpec((2, ROWS, n), lambda i, f: (0, src(i, f), 0)),
        pl.BlockSpec((2, steps, ROWS, n), lambda i, f: (0, 0, src(i, f), 0)),
        pl.BlockSpec((ROWS, n), lambda i, f: (src(i, f), 0)),
        pl.BlockSpec((ROWS, n), lambda i, f: (src(i, f), 0)),
        pl.BlockSpec((2, steps, ROWS, 128), lambda i, f: (0, 0, src(i, f), 0)),
        pl.BlockSpec((2, steps, n), lambda i, f: (0, 0, 0)),
    ]
    args = [flag, enter, noise, keep, filt, ea, eb]
    alias = {}
    if z is not None:
        in_specs.append(pl.BlockSpec(memory_space=pl.ANY))
        args.append(z)
        alias = {7: 0}
    return pl.pallas_call(
        scan_kernel,
        out_shape=(
            jax.ShapeDtypeStruct((2, steps, 2, slab + ROWS, n), BF16),
            jax.ShapeDtypeStruct((2, slab + ROWS, n), BF16),
        ),
        grid_spec=pltpu.PrefetchScalarGridSpec(
            num_scalar_prefetch=1,
            grid=(blocks,),
            in_specs=in_specs,
            out_specs=[
                pl.BlockSpec((2, steps, 2, ROWS, n), lambda i, f: (0, 0, 0, dst(i, f), 0)),
                pl.BlockSpec((2, ROWS, n), lambda i, f: (0, dst(i, f), 0)),
            ],
        ),
        input_output_aliases=alias,
        compiler_params=pltpu.CompilerParams(vmem_limit_bytes=VMEM),
        name="scan",
    )(*args)


def first_kernel(table, z, out):
    owners, parts, frames = out.shape[:3]
    rows = out.shape[3] // 2
    for p in range(2):
        right = z[p].reshape(owners * frames * 128, z.shape[-1])
        acc = lax.dot_general(
            table[p], right, (((1,), (1,)), ((), ())), preferred_element_type=F32
        ).astype(BF16)
        for o in range(owners):
            for f in range(frames):
                c = (o * frames + f) * 128
                out[o, :, f, p * rows : (p + 1) * rows, :] = acc[:, c : c + 128].reshape(
                    parts, rows, 128
                )


def first_call(table, z, chunk, frames, parts, slab):
    n = z.shape[-1]
    group = 8
    return pl.pallas_call(
        first_kernel,
        out_shape=jax.ShapeDtypeStruct((2, parts, frames, slab, 128), BF16),
        grid=(parts // group,),
        in_specs=[
            pl.BlockSpec((2, group * slab // 2, n), lambda i: (0, i, 0)),
            pl.BlockSpec((2, 2, frames, 2, slab, n), lambda i: (0, 0, chunk, 0, 0, 0)),
        ],
        out_specs=pl.BlockSpec((2, group, frames, slab, 128), lambda i: (0, i, 0, 0, 0)),
        compiler_params=pltpu.CompilerParams(vmem_limit_bytes=VMEM),
        cost_estimate=pl.CostEstimate(
            flops=2 * n * n * 2 * frames * 128, bytes_accessed=24 << 20, transcendentals=0
        ),
        name="first",
    )(table, z)


def second_kernel(table, got, *rest):
    out, left, rows = rest[-3:]
    parts, frames, slab = got.shape[1:4]
    half = slab // 2

    @pl.when(pl.program_id(0) == 0)
    def _():
        for m in range(parts):
            both = got[0, m].astype(F32) + got[1, m].astype(F32)
            for f in range(frames):
                for p in range(2):
                    rows[m % 4, pl.ds(f * slab + p, half, stride=2), :] = both[
                        f, p * half : (p + 1) * half
                    ]
            left[:, m * 128 : (m + 1) * 128] = rows[m % 4].astype(BF16)

    acc = jnp.dot(left[...], table[...], preferred_element_type=F32)
    out[...] = acc.reshape(frames, slab, acc.shape[-1])


def second_call(table, got, chunk, total, out=None):
    parts, frames, slab = got.shape[1:4]
    depth, n = table.shape
    tile = 512
    in_specs = [
        pl.BlockSpec((depth, tile), lambda i: (0, i)),
        pl.BlockSpec((2, parts, frames, slab, 128), lambda i: (0, 0, 0, 0, 0)),
    ]
    args = [table, got]
    alias = {}
    if out is not None:
        in_specs.append(pl.BlockSpec(memory_space=pl.ANY))
        args.append(out)
        alias = {2: 0}
    return pl.pallas_call(
        second_kernel,
        out_shape=jax.ShapeDtypeStruct((total, slab, n), F32),
        grid=(n // tile,),
        in_specs=in_specs,
        out_specs=pl.BlockSpec((frames, slab, tile), lambda i: (chunk, 0, i)),
        scratch_shapes=[
            pltpu.VMEM((frames * slab, depth), BF16),
            pltpu.VMEM((4, frames * slab, 128), F32),
        ],
        input_output_aliases=alias,
        compiler_params=pltpu.CompilerParams(vmem_limit_bytes=VMEM),
        cost_estimate=pl.CostEstimate(
            flops=2 * depth * n * frames * slab, bytes_accessed=24 << 20, transcendentals=0
        ),
        name="second",
    )(*args)


CHUNKS = 2


def shards(innovation, retention, rytov_filter, wind_shift, start_state):
    noise = innovation[:, 0]
    keep, filt = retention[0], rytov_filter[0]
    wind = wind_shift[0]
    steps, slab, n = noise.shape[1:]
    parts = lax.axis_size("mode")
    total = steps // 2
    frames = total // CHUNKS
    first, second = tables(n, parts)

    def waves(k):
        return jnp.where(k >= n // 2, k - n, k).astype(F32)

    angle_step = 2.0 * math.pi / n
    rows = lax.axis_index("mode") * slab + lax.iota(jnp.int32, slab)
    pa = wind[:, 0:1] * (waves(rows) * angle_step)[None]
    pb = wind[:, 1:2] * (waves(lax.iota(jnp.int32, n)) * angle_step)[None]
    ea = jnp.broadcast_to(jnp.stack([jnp.cos(pa), jnp.sin(pa)])[..., None], (2, steps, slab, 128))
    eb = jnp.stack([jnp.cos(pb), jnp.sin(pb)])

    core = lax.axis_index("tm").astype(jnp.int32)
    z, last = scan_call((1 - core)[None], start_state[:, 0], noise, keep, filt, ea, eb)
    enter = lax.ppermute(last[:, :slab], "tm", [(0, 1)])
    z, _ = scan_call(core[None], enter, noise, keep, filt, ea, eb, z)
    z = z.reshape(2, 2, total, 2, slab + ROWS, n)

    out = None
    for c in range(CHUNKS):
        part = first_call(first, z, c, frames, parts, slab)
        got = lax.all_to_all(
            part.reshape(2 * parts, frames, slab, 128), ("layer", "mode"), 0, 0, tiled=True
        ).reshape(2, parts, frames, slab, 128)
        out = second_call(second, got, c, total, out)
    return out


def solution(mesh):
    return jax.shard_map(
        shards,
        mesh=mesh,
        in_specs=(
            P(None, "layer", "tm", "mode", None),
            P("layer", "mode", None),
            P("layer", "mode", None),
            P("layer", "tm", None),
            P(None, "layer", "mode", None),
        ),
        out_specs=P(("tm", "layer"), "mode", None),
        check_vma=False,
    )
```

```python
import math

import jax
import jax.numpy as jnp
import numpy as np
from jax import lax
from jax.experimental import pallas as pl
from jax.experimental.pallas import tpu as pltpu
from jax.sharding import PartitionSpec as P

F32, BF16 = jnp.float32, jnp.bfloat16
ROWS = 16
FOLD = 4
CHUNKS = 2
VMEM = 56 * 1024 * 1024


def tables(n, parts):
    k = np.arange(n, dtype=np.int64)
    prod = (k[:, None] * k[None, :]) % n
    ang = np.arange(n, dtype=np.float64) * (2.0 * math.pi / n)
    cos, sin = np.cos(ang)[prod], np.sin(ang)[prod]
    depth, slab = n // FOLD, n // parts
    c, s = cos[:, :depth], sin[:, :depth]
    first = np.stack([np.concatenate([c, -s], 1), np.concatenate([s, c], 1)])
    first = first.reshape(2, n // FOLD, FOLD, 2 * depth).transpose(2, 0, 1, 3)
    both = np.stack([cos[:, : n // 2], -sin[:, : n // 2]]) * (1.0 / n)
    both = both.reshape(2, parts, slab // 2, 2, n // 2).transpose(3, 1, 0, 2, 4)
    second = both.reshape(2, n, n // 2)
    order = np.zeros((2, 2, 2, slab, 2, 2, 2, slab // 2))
    for m in range(2):
        for r in range(2):
            for a in range(slab):
                order[m, :, r, a, a % 2, m, r, a // 2] = 1.0
    order = order.reshape(8 * slab, 4 * slab)
    return first.astype(BF16), second.astype(BF16), order.astype(BF16)


def scan_kernel(flag, enter, noise, keep, filt, ca, sa, cb, sb, *rest):
    z, last, ea = rest[-3:]
    steps, slab, n = noise.shape[1:]
    depth = n // FOLD

    def block(enter, noise, keep, filt, ca, sa, z, last):
        for t in range(steps):
            ea[0, t] = jnp.broadcast_to(ca[:, t : t + 1], (ROWS, 128))
            ea[1, t] = jnp.broadcast_to(sa[:, t : t + 1], (ROWS, 128))

        def lanes(j, carry):
            at = [pl.ds(pl.multiple_of(j * 128 + h * depth, 128), 128) for h in range(FOLD)]
            re = [enter[0, :, c].astype(F32) for c in at]
            im = [enter[1, :, c].astype(F32) for c in at]
            for t in range(steps):
                ar, ai = ea[0, t], ea[1, t]
                tr, ti = [], []
                for h in range(FOLD):
                    br, bi = cb[t : t + 1, at[h]], sb[t : t + 1, at[h]]
                    kp, ft = keep[:, at[h]], filt[:, at[h]]
                    gr = kp * (ar * br - ai * bi)
                    gi = kp * (ar * bi + ai * br)
                    nr = gr * re[h] - gi * im[h] + noise[0, t, :, at[h]].astype(F32)
                    ni = gr * im[h] + gi * re[h] + noise[1, t, :, at[h]].astype(F32)
                    re[h], im[h] = nr, ni
                    tr.append((ft * nr).astype(BF16))
                    ti.append((ft * ni).astype(BF16))
                sr, si = tr[0] + tr[2], ti[0] + ti[2]
                dr, di = tr[0] - tr[2], ti[0] - ti[2]
                ur, ui = tr[1] + tr[3], ti[1] + ti[3]
                vr, vi = tr[1] - tr[3], ti[1] - ti[3]
                z[0, t, :, at[0]], z[0, t, :, at[1]] = sr + ur, si + ui
                z[1, t, :, at[0]], z[1, t, :, at[1]] = dr - vi, di + vr
                z[2, t, :, at[0]], z[2, t, :, at[1]] = sr - ur, si - ui
                z[3, t, :, at[0]], z[3, t, :, at[1]] = dr + vi, di - vr
            for h in range(FOLD):
                last[0, :, at[h]] = re[h].astype(BF16)
                last[1, :, at[h]] = im[h].astype(BF16)
            return carry

        lax.fori_loop(0, depth // 128, lanes, 0)

    @pl.when(flag[0] == 1)
    def _():
        pltpu.emit_pipeline(
            block,
            grid=(slab // ROWS,),
            in_specs=[
                pl.BlockSpec((2, ROWS, n), lambda i: (0, i, 0)),
                pl.BlockSpec((2, steps, ROWS, n), lambda i: (0, 0, i, 0)),
                pl.BlockSpec((ROWS, n), lambda i: (i, 0)),
                pl.BlockSpec((ROWS, n), lambda i: (i, 0)),
                pl.BlockSpec((ROWS, steps), lambda i: (i, 0)),
                pl.BlockSpec((ROWS, steps), lambda i: (i, 0)),
            ],
            out_specs=[
                pl.BlockSpec((FOLD, steps, ROWS, 2 * depth), lambda i: (0, 0, i, 0)),
                pl.BlockSpec((2, ROWS, n), lambda i: (0, i, 0)),
            ],
        )(enter, noise, keep, filt, ca, sa, z, last)


def scan_call(flag, enter, noise, keep, filt, ca, sa, cb, sb, z=None):
    steps, slab, n = noise.shape[1:]
    anywhere = pl.BlockSpec(memory_space=pl.ANY)
    inside = pl.BlockSpec(memory_space=pltpu.VMEM)
    in_specs = [pl.BlockSpec(memory_space=pltpu.SMEM)] + [anywhere] * 6 + [inside] * 2
    args = [flag, enter, noise, keep, filt, ca, sa, cb, sb]
    alias = {}
    if z is not None:
        in_specs.append(anywhere)
        args.append(z)
        alias = {9: 0}
    return pl.pallas_call(
        scan_kernel,
        out_shape=(
            jax.ShapeDtypeStruct((FOLD, steps, slab, 2 * n // FOLD), BF16),
            jax.ShapeDtypeStruct((2, slab, n), BF16),
        ),
        in_specs=in_specs,
        out_specs=[anywhere, anywhere],
        scratch_shapes=[pltpu.VMEM((2, steps, ROWS, 128), F32)],
        input_output_aliases=alias,
        compiler_params=pltpu.CompilerParams(vmem_limit_bytes=VMEM),
        name="scan",
    )(*args)


def first_kernel(table, z, out):
    owners, parts, frames, rows = out.shape[:4]
    slab, depth = z.shape[3:]
    left = table[0].reshape(2 * parts * rows, depth)
    right = z[0].reshape(owners * frames * slab, depth)
    acc = lax.dot_general(
        left, right, (((1,), (1,)), ((), ())), preferred_element_type=F32
    ).astype(BF16)
    re, im = acc[: parts * rows], acc[parts * rows :]
    for o in range(owners):
        for f in range(frames):
            c = (o * frames + f) * slab
            pair = jnp.concatenate([re[:, c : c + slab], im[:, c : c + slab]], axis=1)
            out[o, :, f] = pair.reshape(parts, rows, 2 * slab)


def first_call(table, z, chunk, frames, parts):
    total, slab, depth = z.shape[2:]
    rows = slab // FOLD
    return pl.pallas_call(
        first_kernel,
        out_shape=jax.ShapeDtypeStruct((2, parts, frames, slab, 2 * slab), BF16),
        grid=(FOLD,),
        in_specs=[
            pl.BlockSpec((1, 2, parts * rows, depth), lambda i: (i, 0, 0, 0)),
            pl.BlockSpec((1, 2, frames, slab, depth), lambda i: (i, 0, chunk, 0, 0)),
        ],
        out_specs=pl.BlockSpec((2, parts, frames, rows, 2 * slab), lambda i: (0, 0, 0, i, 0)),
        compiler_params=pltpu.CompilerParams(vmem_limit_bytes=VMEM),
        cost_estimate=pl.CostEstimate(
            flops=16 * frames * parts * slab * slab * depth,
            bytes_accessed=16 << 20,
            transcendentals=0,
        ),
        name="first",
    )(table, z)


def second_kernel(table, order, got, *rest):
    out, left, rows = rest[-3:]
    parts, frames, slab, lanes = got.shape[1:]
    piece = slab // FOLD
    tile = table.shape[2]
    half = out.shape[2] // 2
    step = pl.program_id(0)

    @pl.when(step == 0)
    def _():
        for m in range(0, parts, 2):
            four = [got[l, m + k].reshape(frames * slab, lanes) for k in range(2) for l in range(2)]
            both = jnp.dot(
                jnp.concatenate(four, axis=1), order[...], preferred_element_type=F32
            )
            for p in range(2):
                slot = (m + p) % 4
                for f in range(frames):
                    for q in range(FOLD):
                        a = f * slab + q * piece
                        rows[slot, pl.ds(f * slab + q, piece, stride=FOLD), :] = both[
                            a : a + piece, p * lanes : (p + 1) * lanes
                        ]
                left[p, :, m * slab : (m + 2) * slab] = rows[slot].astype(BF16)

    even = jnp.dot(left[0], table[0], preferred_element_type=F32)
    odd = jnp.dot(left[1], table[1], preferred_element_type=F32)
    lo = pl.multiple_of(step * tile, tile)
    out[:, :, pl.ds(lo, tile)] = (even + odd).reshape(frames, slab, tile)
    out[:, :, pl.ds(pl.multiple_of(lo + half, tile), tile)] = (even - odd).reshape(
        frames, slab, tile
    )


def second_call(table, order, got, chunk, total, out=None):
    parts, frames, slab = got.shape[1:4]
    depth, half = table.shape[1:]
    tile = 256
    in_specs = [
        pl.BlockSpec((2, depth, tile), lambda i: (0, 0, i)),
        pl.BlockSpec(order.shape, lambda i: (0, 0)),
        pl.BlockSpec(got.shape, lambda i: (0, 0, 0, 0, 0)),
    ]
    args = [table, order, got]
    alias = {}
    if out is not None:
        in_specs.append(pl.BlockSpec(memory_space=pl.ANY))
        args.append(out)
        alias = {3: 0}
    return pl.pallas_call(
        second_kernel,
        out_shape=jax.ShapeDtypeStruct((total, slab, 2 * half), F32),
        grid=(half // tile,),
        in_specs=in_specs,
        out_specs=pl.BlockSpec((frames, slab, 2 * half), lambda i: (chunk, 0, 0)),
        scratch_shapes=[
            pltpu.VMEM((2, frames * slab, depth), BF16),
            pltpu.VMEM((4, frames * slab, 2 * slab), F32),
        ],
        input_output_aliases=alias,
        compiler_params=pltpu.CompilerParams(vmem_limit_bytes=VMEM),
        cost_estimate=pl.CostEstimate(
            flops=4 * depth * half * frames * slab, bytes_accessed=16 << 20, transcendentals=0
        ),
        name="second",
    )(*args)


def shards(innovation, retention, rytov_filter, wind_shift, start_state):
    steps, slab, n = innovation.shape[2:]
    noise = innovation.reshape(2, steps, slab, n)
    keep, filt = retention.reshape(slab, n), rytov_filter.reshape(slab, n)
    wind = wind_shift.reshape(steps, 2)
    parts = lax.axis_size("mode")
    total = steps // 2
    frames = total // CHUNKS
    first, second, order = tables(n, parts)

    def waves(k):
        return jnp.where(k >= n // 2, k - n, k).astype(F32)

    angle_step = 2.0 * math.pi / n
    rows = lax.axis_index("mode") * slab + lax.iota(jnp.int32, slab)
    pa = (waves(rows) * angle_step)[:, None] * wind[None, :, 0]
    pb = wind[:, 1:2] * (waves(lax.iota(jnp.int32, n)) * angle_step)[None]
    turns = (jnp.cos(pa), jnp.sin(pa), jnp.cos(pb), jnp.sin(pb))

    core = lax.axis_index("tm").astype(jnp.int32)
    start = start_state.reshape(2, slab, n)
    z, last = scan_call((1 - core)[None], start, noise, keep, filt, *turns)
    enter = lax.ppermute(last, "tm", [(0, 1), (1, 0)])
    z, _ = scan_call(core[None], enter, noise, keep, filt, *turns, z)
    z = z.reshape(FOLD, 2, total, slab, 2 * n // FOLD)

    out = None
    for c in range(CHUNKS):
        part = first_call(first, z, c, frames, parts)
        got = lax.all_to_all(
            part.reshape(2 * parts, frames, slab, 2 * slab), ("layer", "mode"), 0, 0, tiled=True
        ).reshape(2, parts, frames, slab, 2 * slab)
        out = second_call(second, order, got, c, total, out)
    return out


def solution(mesh):
    return jax.shard_map(
        shards,
        mesh=mesh,
        in_specs=(
            P(None, "layer", "tm", "mode", None),
            P("layer", "mode", None),
            P("layer", "mode", None),
            P("layer", "tm", None),
            P(None, "layer", "mode", None),
        ),
        out_specs=P(("tm", "layer"), "mode", None),
        check_vma=False,
    )
```

```python
import functools
import math

import jax
import jax.numpy as jnp
import numpy as np
from jax import lax
from jax.experimental import pallas as pl
from jax.experimental.pallas import tpu as pltpu
from jax.sharding import PartitionSpec as P

F32, BF16 = jnp.float32, jnp.bfloat16
ROWS = 16
FOLD = 4
CLASSES = 8
SPAN = 4
VMEM = 56 * 1024 * 1024


def tables(n, parts):
    k = np.arange(n, dtype=np.int64)
    prod = (k[:, None] * k[None, :]) % n
    ang = np.arange(n, dtype=np.float64) * (2.0 * math.pi / n)
    cos, sin = np.cos(ang)[prod], np.sin(ang)[prod]
    depth, slab = n // CLASSES, n // parts
    c, s = cos[:, :depth], sin[:, :depth]
    first = np.stack([np.concatenate([c, -s], 1), np.concatenate([s, c], 1)])
    first = first.reshape(2, n // CLASSES, CLASSES, 2 * depth).transpose(2, 0, 1, 3)
    both = np.stack([cos[:, : n // 2], -sin[:, : n // 2]]) * (1.0 / n)
    both = both.reshape(2, parts, slab // 2, 2, n // 2).transpose(3, 1, 0, 2, 4)
    second = both.reshape(2, n, n // 2)
    order = np.zeros((2, 2, slab, 2, 2, 2, slab // 2))
    for m in range(2):
        for r in range(2):
            for a in range(slab):
                order[m, r, a, a % 2, m, r, a // 2] = 1.0
    order = order.reshape(4 * slab, 4 * slab)
    return first.astype(BF16), second.astype(BF16), order.astype(BF16)


def wave_kernel(direct, flag, wind, enter, noise, keep, filt, table, *rest):
    (
        part, last, enter_v, noise_v, keep_v, filt_v, table_v, part_v, last_v,
        ea, cb, sb, state, z, zz, sems,
    ) = rest[-16:]
    steps, slab, n = noise.shape[1:]
    parts, frames = part.shape[1], part.shape[3]
    depth = n // FOLD
    blocks = steps // SPAN
    entry = enter if direct else enter_v

    def noise_copy(i):
        at = pl.ds(i * SPAN, SPAN)
        return pltpu.make_async_copy(noise.at[:, at], noise_v.at[:, at], sems.at[4 + i])

    def part_copy(q):
        return pltpu.make_async_copy(part_v.at[q], part.at[:, :, q], sems.at[4 + blocks + q])

    def scan(i, rb):
        rows = pl.ds(pl.multiple_of(rb * ROWS, ROWS), ROWS)
        for j in range(depth // 128):
            at = [slice(j * 128 + h * depth, j * 128 + h * depth + 128) for h in range(FOLD)]
            if i == 0:
                re = [entry[0, rows, c].astype(F32) for c in at]
                im = [entry[1, rows, c].astype(F32) for c in at]
            else:
                re = [state[0, rows, c] for c in at]
                im = [state[1, rows, c] for c in at]
            for s in range(SPAN):
                t = i * SPAN + s
                ar, ai = ea[0, t, rows], ea[1, t, rows]
                tr, ti = [], []
                for h in range(FOLD):
                    br, bi = cb[t : t + 1, at[h]], sb[t : t + 1, at[h]]
                    kp, ft = keep_v[rows, at[h]], filt_v[rows, at[h]]
                    gr = kp * (ar * br - ai * bi)
                    gi = kp * (ar * bi + ai * br)
                    nr = gr * re[h] - gi * im[h] + noise_v[0, t, rows, at[h]].astype(F32)
                    ni = gr * im[h] + gi * re[h] + noise_v[1, t, rows, at[h]].astype(F32)
                    re[h], im[h] = nr, ni
                    tr.append((ft * nr).astype(BF16))
                    ti.append((ft * ni).astype(BF16))
                sr, si = tr[0] + tr[2], ti[0] + ti[2]
                dr, di = tr[0] - tr[2], ti[0] - ti[2]
                ur, ui = tr[1] + tr[3], ti[1] + ti[3]
                vr, vi = tr[1] - tr[3], ti[1] - ti[3]
                z[0, t, rows, at[0]], z[0, t, rows, at[1]] = sr + ur, si + ui
                z[1, t, rows, at[0]], z[1, t, rows, at[1]] = dr - vi, di + vr
                z[2, t, rows, at[0]], z[2, t, rows, at[1]] = sr - ur, si - ui
                z[3, t, rows, at[0]], z[3, t, rows, at[1]] = dr + vi, di - vr
            for h in range(FOLD):
                if i < blocks - 1:
                    state[0, rows, at[h]], state[1, rows, at[h]] = re[h], im[h]
                else:
                    last_v[0, rows, at[h]] = re[h].astype(BF16)
                    last_v[1, rows, at[h]] = im[h].astype(BF16)

    def turns():
        angle = 2.0 * math.pi / n
        lane = lax.broadcasted_iota(jnp.int32, (slab, 128), 1)
        line = lax.broadcasted_iota(jnp.int32, (slab, 128), 0)
        across = jnp.zeros((slab, 128), F32)
        down = jnp.zeros((steps, 128), F32)
        for t in range(steps):
            across = jnp.where(lane == t, wind[0, t], across)
            down = jnp.where(line[:steps] == t, wind[1, t], down)

        def waves(k):
            return jnp.where(k >= n // 2, k - n, k).astype(F32) * angle

        pa = waves(line + flag[1]) * across
        fine = lane[:steps].astype(F32) * angle * down
        coarse = waves(lane[:steps] * 128) * down
        ca, sa = jnp.cos(pa), jnp.sin(pa)
        cq, sq = jnp.cos(fine), jnp.sin(fine)
        cp, sp = jnp.cos(coarse), jnp.sin(coarse)
        for t in range(steps):
            ea[0, t] = jnp.broadcast_to(ca[:, t : t + 1], (slab, 128))
            ea[1, t] = jnp.broadcast_to(sa[:, t : t + 1], (slab, 128))
        for c in range(n // 128):
            x, y = cp[:, c : c + 1], sp[:, c : c + 1]
            cb[:, c * 128 : (c + 1) * 128] = x * cq - y * sq
            sb[:, c * 128 : (c + 1) * 128] = x * sq + y * cq

    def fold(q):
        quarter = depth // 2
        root = jnp.asarray(math.sqrt(0.5), BF16)
        for t in range(steps):
            rows = pl.ds(t * slab, slab)
            lr, hr, li, hi = (z[q, t, :, k * quarter : (k + 1) * quarter] for k in range(4))
            if q == 0:
                wr, wi = hr, hi
            elif q == 1:
                wr, wi = (hr - hi) * root, (hr + hi) * root
            elif q == 2:
                wr, wi = -hi, hr
            else:
                wr, wi = -(hr + hi) * root, (hr - hi) * root
            zz[0, rows, :quarter], zz[0, rows, quarter:] = lr + wr, li + wi
            zz[1, rows, :quarter], zz[1, rows, quarter:] = lr - wr, li - wi

    def transform(q):
        piece = slab // CLASSES
        left = [table_v[q + FOLD * p].reshape(2 * parts * piece, depth) for p in range(2)]
        acc = [
            lax.dot_general(
                left[p], zz[p], (((1,), (1,)), ((), ())), preferred_element_type=F32
            )
            for p in range(2)
        ]
        for o in range(2):
            for f in range(frames):
                c = (o * frames + f) * slab
                both = []
                for p in range(2):
                    re, im = acc[p][: parts * piece], acc[p][parts * piece :]
                    pair = jnp.concatenate([re[:, c : c + slab], im[:, c : c + slab]], axis=1)
                    both.append(pair.reshape(parts, piece, 2 * slab))
                part_v[q, o, :, f] = jnp.concatenate(both, axis=1).astype(BF16)

    @pl.when(flag[0] == 1)
    def _():
        heads = [
            pltpu.make_async_copy(keep, keep_v, sems.at[1]),
            pltpu.make_async_copy(filt, filt_v, sems.at[2]),
        ]
        if not direct:
            heads.append(pltpu.make_async_copy(enter, enter_v, sems.at[0]))
        full = pltpu.make_async_copy(table, table_v, sems.at[3])
        for c in heads:
            c.start()
        noise_copy(0).start()
        noise_copy(1).start()
        full.start()
        for i in range(2, blocks):
            noise_copy(i).start()
        turns()
        for c in heads:
            c.wait()
        for i in range(blocks):
            noise_copy(i).wait()

            def piece(rb, carry):
                scan(i, rb)
                return carry

            lax.fori_loop(0, slab // ROWS, piece, 0)
        final = pltpu.make_async_copy(last_v, last, sems.at[0])
        final.start()
        full.wait()

        for q in range(FOLD):
            fold(q)
            transform(q)
            part_copy(q).start()
        final.wait()
        for q in range(FOLD):
            part_copy(q).wait()


def wave_call(flag, wind, enter, noise, keep, filt, table, parts, part=None):
    steps, slab, n = noise.shape[1:]
    direct = part is not None
    anywhere = pl.BlockSpec(memory_space=pl.ANY)
    inside = pl.BlockSpec(memory_space=pltpu.VMEM)
    scalars = pl.BlockSpec(memory_space=pltpu.SMEM)
    in_specs = [scalars, scalars, inside if direct else anywhere] + [anywhere] * 4
    args = [flag, wind, enter, noise, keep, filt, table]
    alias = {}
    if direct:
        in_specs.append(anywhere)
        args.append(part)
        alias = {7: 0}
    blocks = steps // SPAN
    piece = slab // FOLD
    depth = n // FOLD
    return pl.pallas_call(
        functools.partial(wave_kernel, direct),
        out_shape=(
            jax.ShapeDtypeStruct((2, parts, FOLD, steps // 2, piece, 2 * slab), BF16),
            jax.ShapeDtypeStruct((2, slab, n), BF16),
        ),
        in_specs=in_specs,
        out_specs=[anywhere, anywhere],
        scratch_shapes=[
            pltpu.VMEM((2, 8, 128) if direct else enter.shape, enter.dtype),
            pltpu.VMEM(noise.shape, noise.dtype),
            pltpu.VMEM(keep.shape, F32),
            pltpu.VMEM(filt.shape, F32),
            pltpu.VMEM(table.shape, BF16),
            pltpu.VMEM((FOLD, 2, parts, steps // 2, piece, 2 * slab), BF16),
            pltpu.VMEM((2, slab, n), BF16),
            pltpu.VMEM((2, steps, slab, 128), F32),
            pltpu.VMEM((steps, n), F32),
            pltpu.VMEM((steps, n), F32),
            pltpu.VMEM((2, slab, n), F32),
            pltpu.VMEM((FOLD, steps, slab, 2 * depth), BF16),
            pltpu.VMEM((2, steps * slab, depth), BF16),
            pltpu.SemaphoreType.DMA((4 + blocks + FOLD,)),
        ],
        input_output_aliases=alias,
        compiler_params=pltpu.CompilerParams(vmem_limit_bytes=VMEM),
        name="wave",
    )(*args)


TILE = 512
GATHER = 2


def second_kernel(start, table, order, got, *rest):
    out, left, done, sems = rest[-4:]
    parts, _, frames, piece, lanes = got.shape[1:]
    slab = FOLD * piece
    tile = table.shape[2]
    half = out.shape[2] // 2
    step = pl.program_id(0)

    @pl.when(step < GATHER)
    def _():
        for m in range(0, parts, 2):
            two = [(got[0, m + k] + got[1, m + k]).reshape(frames * slab, lanes) for k in range(2)]
            both = jnp.dot(
                jnp.concatenate(two, axis=1), order[...], preferred_element_type=F32
            )
            at = pl.multiple_of((step * parts + m) * slab, lanes)
            for p in range(2):
                left[p, :, pl.ds(at, lanes)] = both[:, p * lanes : (p + 1) * lanes].astype(BF16)

    def copy(i, h, w):
        lo = pl.multiple_of(i * tile + h * half + w * lanes, lanes)
        return pltpu.make_async_copy(
            done.at[h, i, w], out.at[pl.ds(start, frames), :, pl.ds(lo, lanes)], sems.at[h, i, w]
        )

    tiles = half // tile

    @pl.when(step >= GATHER)
    def _():
        i = step - GATHER
        even = jnp.dot(left[0], table[0], preferred_element_type=F32)
        odd = jnp.dot(left[1], table[1], preferred_element_type=F32)
        for h, both in enumerate((even + odd, even - odd)):
            for w in range(tile // lanes):
                for q in range(FOLD):
                    for f in range(frames):
                        for p in range(2):
                            a = (q * frames + f) * piece + p * piece // 2
                            at = pl.ds(q + FOLD * p, piece // 2, stride=CLASSES)
                            done[h, i, w, f, at, :] = both[
                                a : a + piece // 2, w * lanes : (w + 1) * lanes
                            ]
                copy(i, h, w).start()

    @pl.when(step == GATHER + tiles - 1)
    def _():
        for i in range(tiles):
            for h in range(2):
                for w in range(tile // lanes):
                    copy(i, h, w).wait()


def second_call(table, order, got, start, total, out=None):
    parts, _, frames, piece, lanes = got.shape[1:]
    slab = FOLD * piece
    depth, half = table.shape[1:]
    tile = TILE
    in_specs = [
        pl.BlockSpec((2, depth, tile), lambda i: (0, 0, jnp.maximum(i - GATHER, 0))),
        pl.BlockSpec(order.shape, lambda i: (0, 0)),
        pl.BlockSpec(
            (2, parts // GATHER, FOLD, frames, piece, lanes),
            lambda i: (0, jnp.minimum(i, GATHER - 1), 0, 0, 0, 0),
        ),
    ]
    args = [table, order, got]
    alias = {}
    if out is not None:
        in_specs.append(pl.BlockSpec(memory_space=pl.ANY))
        args.append(out)
        alias = {3: 0}
    return pl.pallas_call(
        functools.partial(second_kernel, start),
        out_shape=jax.ShapeDtypeStruct((total, slab, 2 * half), F32),
        grid=(GATHER + half // tile,),
        in_specs=in_specs,
        out_specs=pl.BlockSpec(memory_space=pl.ANY),
        scratch_shapes=[
            pltpu.VMEM((2, frames * slab, depth), BF16),
            pltpu.VMEM((2, half // tile, tile // lanes, frames, slab, lanes), F32),
            pltpu.SemaphoreType.DMA((2, half // tile, tile // lanes)),
        ],
        input_output_aliases=alias,
        compiler_params=pltpu.CompilerParams(vmem_limit_bytes=VMEM),
        cost_estimate=pl.CostEstimate(
            flops=4 * depth * half * frames * slab, bytes_accessed=20 << 20, transcendentals=0
        ),
        name="second",
    )(*args)


def shards(innovation, retention, rytov_filter, wind_shift, start_state):
    steps, slab, n = innovation.shape[2:]
    noise = innovation.reshape(2, steps, slab, n)
    keep, filt = retention.reshape(slab, n), rytov_filter.reshape(slab, n)
    wind = wind_shift.reshape(steps, 2).T
    parts = lax.axis_size("mode")
    first, second, order = tables(n, parts)

    core = lax.axis_index("tm").astype(jnp.int32)
    row = lax.axis_index("mode").astype(jnp.int32) * slab
    start = start_state.reshape(2, slab, n)
    flags = [jnp.stack([on, row]) for on in (1 - core, core)]
    part, last = wave_call(flags[0], wind, start, noise, keep, filt, first, parts)
    enter = lax.ppermute(last, "tm", [(0, 1), (1, 0)])
    part, _ = wave_call(flags[1], wind, enter, noise, keep, filt, first, parts, part)
    got = lax.all_to_all(
        part.reshape((2 * parts,) + part.shape[2:]), ("layer", "mode"), 0, 0, tiled=True
    ).reshape(part.shape)
    return second_call(second, order, got, 0, steps // 2)


def solution(mesh):
    return jax.shard_map(
        shards,
        mesh=mesh,
        in_specs=(
            P(None, "layer", "tm", "mode", None),
            P("layer", "mode", None),
            P("layer", "mode", None),
            P("layer", "tm", None),
            P(None, "layer", "mode", None),
        ),
        out_specs=P(("tm", "layer"), "mode", None),
        check_vma=False,
    )
```

```python
import functools
import math

import jax
import jax.numpy as jnp
import numpy as np
from jax import lax
from jax.experimental import pallas as pl
from jax.experimental.pallas import tpu as pltpu
from jax.sharding import PartitionSpec as P

F32, BF16 = jnp.float32, jnp.bfloat16
ROWS = 16
FOLD = 4
CLASSES = 8
SPAN = 4
VMEM = 56 * 1024 * 1024


def tables(n, parts):
    k = np.arange(n, dtype=np.int64)
    prod = (k[:, None] * k[None, :]) % n
    ang = np.arange(n, dtype=np.float64) * (2.0 * math.pi / n)
    cos, sin = np.cos(ang)[prod], np.sin(ang)[prod]
    depth, slab = n // CLASSES, n // parts
    c, s = cos[:, :depth], sin[:, :depth]
    first = np.stack([np.concatenate([c, -s], 1), np.concatenate([s, c], 1)])
    first = first.reshape(2, n // CLASSES, CLASSES, 2 * depth).transpose(2, 0, 1, 3)
    both = np.stack([cos[:, : n // 2], -sin[:, : n // 2]]) * (1.0 / n)
    both = both.reshape(2, parts, slab // 2, 2, n // 2).transpose(3, 1, 0, 2, 4)
    second = both.reshape(2, n, -1, TILE).transpose(2, 0, 1, 3)
    order = np.zeros((2, 2, slab, 2, 2, 2, slab // 2))
    for m in range(2):
        for r in range(2):
            for a in range(slab):
                order[m, r, a, a % 2, m, r, a // 2] = 1.0
    order = order.reshape(4 * slab, 4 * slab)
    return first.astype(BF16), second.astype(BF16), order.astype(BF16)


def wave_kernel(turn, core, row, wind, enter, noise, keep, filt, table, *rest):
    (
        part, last, enter_v, noise_v, keep_v, filt_v, table_v, part_v, last_v,
        ea, cb, sb, state, z, zz, sems,
    ) = rest[-16:]
    steps, slab, n = noise.shape[1:]
    parts, frames = part.shape[1], part.shape[3]
    depth = n // FOLD
    blocks = steps // SPAN

    def noise_copy(i):
        at = pl.ds(i * SPAN, SPAN)
        return pltpu.make_async_copy(noise.at[:, at], noise_v.at[:, at], sems.at[5 + i])

    def part_copy(q):
        return pltpu.make_async_copy(part_v.at[q], part.at[:, :, q], sems.at[5 + blocks + q])

    def scan(i, rb):
        rows = pl.ds(pl.multiple_of(rb * ROWS, ROWS), ROWS)
        for j in range(depth // 128):
            at = [slice(j * 128 + h * depth, j * 128 + h * depth + 128) for h in range(FOLD)]
            if i == 0:
                re = [enter_v[0, rows, c].astype(F32) for c in at]
                im = [enter_v[1, rows, c].astype(F32) for c in at]
            else:
                re = [state[0, rows, c] for c in at]
                im = [state[1, rows, c] for c in at]
            for s in range(SPAN):
                t = i * SPAN + s
                ar, ai = ea[0, t, rows], ea[1, t, rows]
                tr, ti = [], []
                for h in range(FOLD):
                    br, bi = cb[t : t + 1, at[h]], sb[t : t + 1, at[h]]
                    kp, ft = keep_v[rows, at[h]], filt_v[rows, at[h]]
                    gr = kp * (ar * br - ai * bi)
                    gi = kp * (ar * bi + ai * br)
                    nr = gr * re[h] - gi * im[h] + noise_v[0, t, rows, at[h]].astype(F32)
                    ni = gr * im[h] + gi * re[h] + noise_v[1, t, rows, at[h]].astype(F32)
                    re[h], im[h] = nr, ni
                    tr.append((ft * nr).astype(BF16))
                    ti.append((ft * ni).astype(BF16))
                sr, si = tr[0] + tr[2], ti[0] + ti[2]
                dr, di = tr[0] - tr[2], ti[0] - ti[2]
                ur, ui = tr[1] + tr[3], ti[1] + ti[3]
                vr, vi = tr[1] - tr[3], ti[1] - ti[3]
                z[0, t, rows, at[0]], z[0, t, rows, at[1]] = sr + ur, si + ui
                z[1, t, rows, at[0]], z[1, t, rows, at[1]] = dr - vi, di + vr
                z[2, t, rows, at[0]], z[2, t, rows, at[1]] = sr - ur, si - ui
                z[3, t, rows, at[0]], z[3, t, rows, at[1]] = dr + vi, di - vr
            for h in range(FOLD):
                if i < blocks - 1:
                    state[0, rows, at[h]], state[1, rows, at[h]] = re[h], im[h]
                else:
                    last_v[0, rows, at[h]] = re[h].astype(BF16)
                    last_v[1, rows, at[h]] = im[h].astype(BF16)

    def turns():
        angle = 2.0 * math.pi / n
        lane = lax.broadcasted_iota(jnp.int32, (slab, 128), 1)
        line = lax.broadcasted_iota(jnp.int32, (slab, 128), 0)
        across = jnp.zeros((slab, 128), F32)
        down = jnp.zeros((steps, 128), F32)
        for t in range(steps):
            across = jnp.where(lane == t, wind[0, t], across)
            down = jnp.where(line[:steps] == t, wind[1, t], down)

        def waves(k):
            return jnp.where(k >= n // 2, k - n, k).astype(F32) * angle

        pa = waves(line + row[0]) * across
        fine = lane[:steps].astype(F32) * angle * down
        coarse = waves(lane[:steps] * 128) * down
        ca, sa = jnp.cos(pa), jnp.sin(pa)
        cq, sq = jnp.cos(fine), jnp.sin(fine)
        cp, sp = jnp.cos(coarse), jnp.sin(coarse)
        for t in range(steps):
            ea[0, t] = jnp.broadcast_to(ca[:, t : t + 1], (slab, 128))
            ea[1, t] = jnp.broadcast_to(sa[:, t : t + 1], (slab, 128))
        for c in range(n // 128):
            x, y = cp[:, c : c + 1], sp[:, c : c + 1]
            cb[:, c * 128 : (c + 1) * 128] = x * cq - y * sq
            sb[:, c * 128 : (c + 1) * 128] = x * sq + y * cq

    def fold(q):
        quarter = depth // 2
        root = jnp.asarray(math.sqrt(0.5), BF16)
        for t in range(steps):
            rows = pl.ds(t * slab, slab)
            lr, hr, li, hi = (z[q, t, :, k * quarter : (k + 1) * quarter] for k in range(4))
            if q == 0:
                wr, wi = hr, hi
            elif q == 1:
                wr, wi = (hr - hi) * root, (hr + hi) * root
            elif q == 2:
                wr, wi = -hi, hr
            else:
                wr, wi = -(hr + hi) * root, (hr - hi) * root
            zz[0, rows, :quarter], zz[0, rows, quarter:] = lr + wr, li + wi
            zz[1, rows, :quarter], zz[1, rows, quarter:] = lr - wr, li - wi

    def transform(q):
        piece = slab // CLASSES
        left = [table_v[q + FOLD * p].reshape(2 * parts * piece, depth) for p in range(2)]
        acc = [
            lax.dot_general(
                left[p], zz[p], (((1,), (1,)), ((), ())), preferred_element_type=F32
            )
            for p in range(2)
        ]
        for o in range(2):
            for f in range(frames):
                c = (o * frames + f) * slab
                both = []
                for p in range(2):
                    re, im = acc[p][: parts * piece], acc[p][parts * piece :]
                    pair = jnp.concatenate([re[:, c : c + slab], im[:, c : c + slab]], axis=1)
                    both.append(pair.reshape(parts, piece, 2 * slab))
                part_v[q, o, :, f] = jnp.concatenate(both, axis=1).astype(BF16)

    @pl.when(core[0] == turn)
    def _():
        heads = [
            pltpu.make_async_copy(keep, keep_v, sems.at[2]),
            pltpu.make_async_copy(filt, filt_v, sems.at[3]),
            pltpu.make_async_copy(enter, enter_v, sems.at[4]),
        ]
        full = pltpu.make_async_copy(table, table_v, sems.at[1])
        for c in heads:
            c.start()
        noise_copy(0).start()
        noise_copy(1).start()
        full.start()
        for i in range(2, blocks):
            noise_copy(i).start()
        turns()
        for c in heads:
            c.wait()
        for i in range(blocks):
            noise_copy(i).wait()

            def piece(rb, carry):
                scan(i, rb)
                return carry

            lax.fori_loop(0, slab // ROWS, piece, 0)
        final = pltpu.make_async_copy(last_v, last, sems.at[0])
        final.start()
        full.wait()

        for q in range(FOLD):
            fold(q)
            transform(q)
            part_copy(q).start()
        final.wait()
        for q in range(FOLD):
            part_copy(q).wait()


def wave_call(turn, core, row, wind, enter, noise, keep, filt, table, parts, part=None):
    steps, slab, n = noise.shape[1:]
    anywhere = pl.BlockSpec(memory_space=pl.ANY)
    in_specs = [pl.BlockSpec(memory_space=pltpu.SMEM)] * 3 + [anywhere] * 5
    args = [core, row, wind, enter, noise, keep, filt, table]
    alias = {}
    if part is not None:
        in_specs.append(anywhere)
        args.append(part)
        alias = {8: 0}
    blocks = steps // SPAN
    piece = slab // FOLD
    depth = n // FOLD
    return pl.pallas_call(
        functools.partial(wave_kernel, turn),
        out_shape=(
            jax.ShapeDtypeStruct((2, parts, FOLD, steps // 2, piece, 2 * slab), BF16),
            jax.ShapeDtypeStruct((2, slab, n), BF16),
        ),
        in_specs=in_specs,
        out_specs=[anywhere, anywhere],
        scratch_shapes=[
            pltpu.VMEM(enter.shape, enter.dtype),
            pltpu.VMEM(noise.shape, noise.dtype),
            pltpu.VMEM(keep.shape, F32),
            pltpu.VMEM(filt.shape, F32),
            pltpu.VMEM(table.shape, BF16),
            pltpu.VMEM((FOLD, 2, parts, steps // 2, piece, 2 * slab), BF16),
            pltpu.VMEM((2, slab, n), BF16),
            pltpu.VMEM((2, steps, slab, 128), F32),
            pltpu.VMEM((steps, n), F32),
            pltpu.VMEM((steps, n), F32),
            pltpu.VMEM((2, slab, n), F32),
            pltpu.VMEM((FOLD, steps, slab, 2 * depth), BF16),
            pltpu.VMEM((2, steps * slab, depth), BF16),
            pltpu.SemaphoreType.DMA((5 + blocks + FOLD,)),
        ],
        input_output_aliases=alias,
        compiler_params=pltpu.CompilerParams(vmem_limit_bytes=VMEM),
        name="wave",
    )(*args)


TILE = 256
GATHER = 4


def second_kernel(table, order, got, out, got_v, left, done, sems):
    parts, _, frames, piece, lanes = got.shape[1:]
    slab = FOLD * piece
    half = out.shape[2] // 2
    tiles = half // TILE
    some = parts // GATHER

    def take(g):
        at = pl.ds(g * some, some)
        return pltpu.make_async_copy(got.at[:, at], got_v.at[:, at], sems.at[g])

    def give(i, h, w):
        lo = i * TILE + h * half + w * lanes
        return pltpu.make_async_copy(
            done.at[h, i, w], out.at[:, :, pl.ds(lo, lanes)], sems.at[GATHER + tiles + (h * tiles + i) * (TILE // lanes) + w]
        )

    for g in range(GATHER):
        take(g).start()
    for g in range(GATHER):
        take(g).wait()
        for m in range(g * some, (g + 1) * some, 2):
            two = [
                (got_v[0, m + k] + got_v[1, m + k]).reshape(frames * slab, lanes)
                for k in range(2)
            ]
            both = jnp.dot(
                jnp.concatenate(two, axis=1), order[...], preferred_element_type=F32
            ).astype(BF16)
            for p in range(2):
                left[p, :, m * slab : (m + 2) * slab] = both[:, p * lanes : (p + 1) * lanes]
    for i in range(tiles):
        even = jnp.dot(left[0], table[i, 0], preferred_element_type=F32)
        odd = jnp.dot(left[1], table[i, 1], preferred_element_type=F32)
        for h, both in enumerate((even + odd, even - odd)):
            for w in range(TILE // lanes):
                for q in range(FOLD):
                    for f in range(frames):
                        for p in range(2):
                            a = (q * frames + f) * piece + p * piece // 2
                            at = pl.ds(q + FOLD * p, piece // 2, stride=CLASSES)
                            done[h, i, w, f, at, :] = both[
                                a : a + piece // 2, w * lanes : (w + 1) * lanes
                            ]
                give(i, h, w).start()
    for i in range(tiles):
        for h in range(2):
            for w in range(TILE // lanes):
                give(i, h, w).wait()


def second_call(table, order, got):
    parts, _, frames, piece, lanes = got.shape[1:]
    slab = FOLD * piece
    tiles, _, depth, _ = table.shape
    half = tiles * TILE
    anywhere = pl.BlockSpec(memory_space=pl.ANY)
    inside = pl.BlockSpec(memory_space=pltpu.VMEM)
    return pl.pallas_call(
        second_kernel,
        out_shape=jax.ShapeDtypeStruct((frames, slab, 2 * half), F32),
        in_specs=[inside, inside, anywhere],
        out_specs=anywhere,
        scratch_shapes=[
            pltpu.VMEM(got.shape, BF16),
            pltpu.VMEM((2, frames * slab, depth), BF16),
            pltpu.VMEM((2, tiles, TILE // lanes, frames, slab, lanes), F32),
            pltpu.SemaphoreType.DMA((GATHER + tiles + 2 * half // lanes,)),
        ],
        compiler_params=pltpu.CompilerParams(vmem_limit_bytes=26 * 1024 * 1024),
        name="second",
    )(table, order, got)


def shards(innovation, retention, rytov_filter, wind_shift, start_state):
    steps, slab, n = innovation.shape[2:]
    noise = innovation.reshape(2, steps, slab, n)
    keep, filt = retention.reshape(slab, n), rytov_filter.reshape(slab, n)
    wind = wind_shift.reshape(steps, 2).T
    parts = lax.axis_size("mode")
    first, second, order = tables(n, parts)

    start = start_state.reshape(2, slab, n)
    core = lax.axis_index("tm").astype(jnp.int32)[None]
    row = (lax.axis_index("mode").astype(jnp.int32) * slab)[None]
    part, last = wave_call(0, core, row, wind, start, noise, keep, filt, first, parts)
    enter = lax.ppermute(last, "tm", [(0, 1), (1, 0)])
    part, _ = wave_call(1, core, row, wind, enter, noise, keep, filt, first, parts, part)
    got = lax.all_to_all(
        part.reshape((2 * parts,) + part.shape[2:]), ("layer", "mode"), 0, 0, tiled=True
    ).reshape(part.shape)
    return second_call(second, order, got)


def solution(mesh):
    return jax.shard_map(
        shards,
        mesh=mesh,
        in_specs=(
            P(None, "layer", "tm", "mode", None),
            P("layer", "mode", None),
            P("layer", "mode", None),
            P("layer", "tm", None),
            P(None, "layer", "mode", None),
        ),
        out_specs=P(("tm", "layer"), "mode", None),
        check_vma=False,
    )
```

```python
import functools
import math

import jax
import jax.numpy as jnp
import numpy as np
from jax import lax
from jax.experimental import pallas as pl
from jax.experimental.pallas import tpu as pltpu
from jax.sharding import PartitionSpec as P

F32, BF16 = jnp.float32, jnp.bfloat16
ROWS = 16
FOLD = 4
CLASSES = 8
SPAN = 4
VMEM = 56 * 1024 * 1024


def tables(n, parts):
    k = np.arange(n, dtype=np.int64)
    prod = (k[:, None] * k[None, :]) % n
    ang = np.arange(n, dtype=np.float64) * (2.0 * math.pi / n)
    cos, sin = np.cos(ang)[prod], np.sin(ang)[prod]
    depth, slab = n // CLASSES, n // parts
    c, s = cos[:, :depth], sin[:, :depth]
    first = np.stack([np.concatenate([c, -s], 1), np.concatenate([s, c], 1)])
    first = first.reshape(2, n // CLASSES, CLASSES, 2 * depth).transpose(2, 0, 1, 3)
    both = np.stack([cos[:, : n // 2], -sin[:, : n // 2]]) * (1.0 / n)
    both = both.reshape(2, parts, slab // 2, 2, n // 2).transpose(3, 1, 0, 2, 4)
    second = both.reshape(2, n, -1, TILE).transpose(2, 0, 1, 3)
    order = np.zeros((2, 2, slab, 2, 2, 2, slab // 2))
    for m in range(2):
        for r in range(2):
            for a in range(slab):
                order[m, r, a, a % 2, m, r, a // 2] = 1.0
    order = order.reshape(4 * slab, 4 * slab)
    return first.astype(BF16), second.astype(BF16), order.astype(BF16)


def wave_kernel(turn, core, row, wind, enter, noise, keep, filt, table, *rest):
    (
        part, last, enter_v, noise_v, keep_v, filt_v, table_v, part_v, last_v,
        ea, cb, sb, state, z, zz, sems,
    ) = rest[-16:]
    steps, slab, n = noise.shape[1:]
    parts, frames = part.shape[1], part.shape[3]
    depth = n // FOLD
    blocks = steps // SPAN

    def noise_copy(i):
        at = pl.ds(i * SPAN, SPAN)
        return pltpu.make_async_copy(noise.at[:, at], noise_v.at[:, at], sems.at[5 + i])

    def part_copy(q):
        return pltpu.make_async_copy(part_v.at[q], part.at[:, :, q], sems.at[5 + blocks + q])

    def scan(i, rb):
        rows = pl.ds(pl.multiple_of(rb * ROWS, ROWS), ROWS)
        for j in range(depth // 128):
            at = [slice(j * 128 + h * depth, j * 128 + h * depth + 128) for h in range(FOLD)]
            if i == 0:
                re = [enter_v[0, rows, c].astype(F32) for c in at]
                im = [enter_v[1, rows, c].astype(F32) for c in at]
            else:
                re = [state[0, rows, c] for c in at]
                im = [state[1, rows, c] for c in at]
            for s in range(SPAN):
                t = i * SPAN + s
                ar, ai = ea[0, t, rows], ea[1, t, rows]
                tr, ti = [], []
                for h in range(FOLD):
                    br, bi = cb[t : t + 1, at[h]], sb[t : t + 1, at[h]]
                    kp, ft = keep_v[rows, at[h]], filt_v[rows, at[h]]
                    gr = kp * (ar * br - ai * bi)
                    gi = kp * (ar * bi + ai * br)
                    nr = gr * re[h] - gi * im[h] + noise_v[0, t, rows, at[h]].astype(F32)
                    ni = gr * im[h] + gi * re[h] + noise_v[1, t, rows, at[h]].astype(F32)
                    re[h], im[h] = nr, ni
                    tr.append((ft * nr).astype(BF16))
                    ti.append((ft * ni).astype(BF16))
                sr, si = tr[0] + tr[2], ti[0] + ti[2]
                dr, di = tr[0] - tr[2], ti[0] - ti[2]
                ur, ui = tr[1] + tr[3], ti[1] + ti[3]
                vr, vi = tr[1] - tr[3], ti[1] - ti[3]
                z[0, t, rows, at[0]], z[0, t, rows, at[1]] = sr + ur, si + ui
                z[1, t, rows, at[0]], z[1, t, rows, at[1]] = dr - vi, di + vr
                z[2, t, rows, at[0]], z[2, t, rows, at[1]] = sr - ur, si - ui
                z[3, t, rows, at[0]], z[3, t, rows, at[1]] = dr + vi, di - vr
            for h in range(FOLD):
                if i < blocks - 1:
                    state[0, rows, at[h]], state[1, rows, at[h]] = re[h], im[h]
                else:
                    last_v[0, rows, at[h]] = re[h].astype(BF16)
                    last_v[1, rows, at[h]] = im[h].astype(BF16)

    def turns():
        angle = 2.0 * math.pi / n
        lane = lax.broadcasted_iota(jnp.int32, (slab, 128), 1)
        line = lax.broadcasted_iota(jnp.int32, (slab, 128), 0)
        across = jnp.zeros((slab, 128), F32)
        down = jnp.zeros((steps, 128), F32)
        for t in range(steps):
            across = jnp.where(lane == t, wind[0, t], across)
            down = jnp.where(line[:steps] == t, wind[1, t], down)

        def waves(k):
            return jnp.where(k >= n // 2, k - n, k).astype(F32) * angle

        pa = waves(line + row[0]) * across
        fine = lane[:steps].astype(F32) * angle * down
        coarse = waves(lane[:steps] * 128) * down
        ca, sa = jnp.cos(pa), jnp.sin(pa)
        cq, sq = jnp.cos(fine), jnp.sin(fine)
        cp, sp = jnp.cos(coarse), jnp.sin(coarse)
        for t in range(steps):
            ea[0, t] = jnp.broadcast_to(ca[:, t : t + 1], (slab, 128))
            ea[1, t] = jnp.broadcast_to(sa[:, t : t + 1], (slab, 128))
        for c in range(n // 128):
            x, y = cp[:, c : c + 1], sp[:, c : c + 1]
            cb[:, c * 128 : (c + 1) * 128] = x * cq - y * sq
            sb[:, c * 128 : (c + 1) * 128] = x * sq + y * cq

    def fold(q):
        quarter = depth // 2
        root = jnp.asarray(math.sqrt(0.5), BF16)
        for t in range(steps):
            rows = pl.ds(t * slab, slab)
            lr, hr, li, hi = (z[q, t, :, k * quarter : (k + 1) * quarter] for k in range(4))
            if q == 0:
                wr, wi = hr, hi
            elif q == 1:
                wr, wi = (hr - hi) * root, (hr + hi) * root
            elif q == 2:
                wr, wi = -hi, hr
            else:
                wr, wi = -(hr + hi) * root, (hr - hi) * root
            zz[0, rows, :quarter], zz[0, rows, quarter:] = lr + wr, li + wi
            zz[1, rows, :quarter], zz[1, rows, quarter:] = lr - wr, li - wi

    def transform(q):
        piece = slab // CLASSES
        left = [table_v[q + FOLD * p].reshape(2 * parts * piece, depth) for p in range(2)]
        acc = [
            lax.dot_general(
                left[p], zz[p], (((1,), (1,)), ((), ())), preferred_element_type=F32
            )
            for p in range(2)
        ]
        for o in range(2):
            for f in range(frames):
                c = (o * frames + f) * slab
                both = []
                for p in range(2):
                    re, im = acc[p][: parts * piece], acc[p][parts * piece :]
                    pair = jnp.concatenate([re[:, c : c + slab], im[:, c : c + slab]], axis=1)
                    both.append(pair.reshape(parts, piece, 2 * slab))
                part_v[q, o, :, f] = jnp.concatenate(both, axis=1).astype(BF16)

    @pl.when(core[0] == turn)
    def _():
        heads = [
            pltpu.make_async_copy(keep, keep_v, sems.at[2]),
            pltpu.make_async_copy(filt, filt_v, sems.at[3]),
            pltpu.make_async_copy(enter, enter_v, sems.at[4]),
        ]
        full = pltpu.make_async_copy(table, table_v, sems.at[1])
        for c in heads:
            c.start()
        noise_copy(0).start()
        noise_copy(1).start()
        for i in range(2, blocks):
            noise_copy(i).start()
        full.start()
        turns()
        for c in heads:
            c.wait()
        for i in range(blocks):
            noise_copy(i).wait()

            def piece(rb, carry):
                scan(i, rb)
                return carry

            lax.fori_loop(0, slab // ROWS, piece, 0)
        final = pltpu.make_async_copy(last_v, last, sems.at[0])
        final.start()
        full.wait()

        for q in range(FOLD):
            fold(q)
            transform(q)
            part_copy(q).start()
        final.wait()
        for q in range(FOLD):
            part_copy(q).wait()


def wave_call(turn, core, row, wind, enter, noise, keep, filt, table, parts, part=None):
    steps, slab, n = noise.shape[1:]
    anywhere = pl.BlockSpec(memory_space=pl.ANY)
    in_specs = [pl.BlockSpec(memory_space=pltpu.SMEM)] * 3 + [anywhere] * 5
    args = [core, row, wind, enter, noise, keep, filt, table]
    alias = {}
    if part is not None:
        in_specs.append(anywhere)
        args.append(part)
        alias = {8: 0}
    blocks = steps // SPAN
    piece = slab // FOLD
    depth = n // FOLD
    return pl.pallas_call(
        functools.partial(wave_kernel, turn),
        out_shape=(
            jax.ShapeDtypeStruct((2, parts, FOLD, steps // 2, piece, 2 * slab), BF16),
            jax.ShapeDtypeStruct((2, slab, n), BF16),
        ),
        in_specs=in_specs,
        out_specs=[anywhere, anywhere],
        scratch_shapes=[
            pltpu.VMEM(enter.shape, enter.dtype),
            pltpu.VMEM(noise.shape, noise.dtype),
            pltpu.VMEM(keep.shape, F32),
            pltpu.VMEM(filt.shape, F32),
            pltpu.VMEM(table.shape, BF16),
            pltpu.VMEM((FOLD, 2, parts, steps // 2, piece, 2 * slab), BF16),
            pltpu.VMEM((2, slab, n), BF16),
            pltpu.VMEM((2, steps, slab, 128), F32),
            pltpu.VMEM((steps, n), F32),
            pltpu.VMEM((steps, n), F32),
            pltpu.VMEM((2, slab, n), F32),
            pltpu.VMEM((FOLD, steps, slab, 2 * depth), BF16),
            pltpu.VMEM((2, steps * slab, depth), BF16),
            pltpu.SemaphoreType.DMA((5 + blocks + FOLD,)),
        ],
        input_output_aliases=alias,
        compiler_params=pltpu.CompilerParams(vmem_limit_bytes=VMEM),
        name="wave",
    )(*args)


TILE = 256
GATHER = 2


def second_kernel(table, order, got, out, got_v, left, done, sems):
    parts, _, frames, piece, lanes = got.shape[1:]
    slab = FOLD * piece
    half = out.shape[2] // 2
    tiles = half // TILE
    some = parts // GATHER

    def take(g):
        at = pl.ds(g * some, some)
        return pltpu.make_async_copy(got.at[:, at], got_v.at[:, at], sems.at[g])

    def give(i, h, w):
        lo = i * TILE + h * half + w * lanes
        return pltpu.make_async_copy(
            done.at[h, i, w], out.at[:, :, pl.ds(lo, lanes)], sems.at[GATHER + tiles + (h * tiles + i) * (TILE // lanes) + w]
        )

    for g in range(GATHER):
        take(g).start()
    for g in range(GATHER):
        take(g).wait()
        for m in range(g * some, (g + 1) * some, 2):
            two = [
                (got_v[0, m + k] + got_v[1, m + k]).reshape(frames * slab, lanes)
                for k in range(2)
            ]
            both = jnp.dot(
                jnp.concatenate(two, axis=1), order[...], preferred_element_type=F32
            ).astype(BF16)
            for p in range(2):
                left[p, :, m * slab : (m + 2) * slab] = both[:, p * lanes : (p + 1) * lanes]
    for i in range(tiles):
        even = jnp.dot(left[0], table[i, 0], preferred_element_type=F32)
        odd = jnp.dot(left[1], table[i, 1], preferred_element_type=F32)
        for h, both in enumerate((even + odd, even - odd)):
            for w in range(TILE // lanes):
                for q in range(FOLD):
                    for f in range(frames):
                        for p in range(2):
                            a = (q * frames + f) * piece + p * piece // 2
                            at = pl.ds(q + FOLD * p, piece // 2, stride=CLASSES)
                            done[h, i, w, f, at, :] = both[
                                a : a + piece // 2, w * lanes : (w + 1) * lanes
                            ]
                give(i, h, w).start()
    for i in range(tiles):
        for h in range(2):
            for w in range(TILE // lanes):
                give(i, h, w).wait()


def second_call(table, order, got):
    parts, _, frames, piece, lanes = got.shape[1:]
    slab = FOLD * piece
    tiles, _, depth, _ = table.shape
    half = tiles * TILE
    anywhere = pl.BlockSpec(memory_space=pl.ANY)
    inside = pl.BlockSpec(memory_space=pltpu.VMEM)
    return pl.pallas_call(
        second_kernel,
        out_shape=jax.ShapeDtypeStruct((frames, slab, 2 * half), F32),
        in_specs=[inside, inside, anywhere],
        out_specs=anywhere,
        scratch_shapes=[
            pltpu.VMEM(got.shape, BF16),
            pltpu.VMEM((2, frames * slab, depth), BF16),
            pltpu.VMEM((2, tiles, TILE // lanes, frames, slab, lanes), F32),
            pltpu.SemaphoreType.DMA((GATHER + tiles + 2 * half // lanes,)),
        ],
        compiler_params=pltpu.CompilerParams(vmem_limit_bytes=26 * 1024 * 1024),
        name="second",
    )(table, order, got)


def shards(innovation, retention, rytov_filter, wind_shift, start_state):
    steps, slab, n = innovation.shape[2:]
    noise = innovation.reshape(2, steps, slab, n)
    keep, filt = retention.reshape(slab, n), rytov_filter.reshape(slab, n)
    wind = wind_shift.reshape(steps, 2).T
    parts = lax.axis_size("mode")
    first, second, order = tables(n, parts)

    start = start_state.reshape(2, slab, n)
    core = lax.axis_index("tm").astype(jnp.int32)[None]
    row = (lax.axis_index("mode").astype(jnp.int32) * slab)[None]
    part, last = wave_call(0, core, row, wind, start, noise, keep, filt, first, parts)
    enter = lax.ppermute(last, "tm", [(0, 1), (1, 0)])
    part, _ = wave_call(1, core, row, wind, enter, noise, keep, filt, first, parts, part)
    got = lax.all_to_all(
        part.reshape((2 * parts,) + part.shape[2:]), ("layer", "mode"), 0, 0, tiled=True
    ).reshape(part.shape)
    return second_call(second, order, got)


def solution(mesh):
    return jax.shard_map(
        shards,
        mesh=mesh,
        in_specs=(
            P(None, "layer", "tm", "mode", None),
            P("layer", "mode", None),
            P("layer", "mode", None),
            P("layer", "tm", None),
            P(None, "layer", "mode", None),
        ),
        out_specs=P(("tm", "layer"), "mode", None),
        check_vma=False,
    )
```
